32 devices in a mesh: brick: 8 (over z, y), level: 4 (over x, core).
Axes of the slice: x: 2, y: 2, z: 4, core: 2. Of those that a mesh axis runs over, the one named last changes fastest.
Arguments:
- adjoint: float32 [5, 32, 64, 128], P(None, 'level', 'brick'), may hold values from -6 to 6
- source: float32 [5, 32, 64, 128], P(None, 'level', 'brick'), may hold values from -48 to 48
- block: bfloat16 [5, 5, 32, 64, 128], P(None, None, 'level', 'brick'), may hold values from -1 to 13
- precond: bfloat16 [5, 5, 32, 64, 128], P(None, None, 'level', 'brick'), may hold values from -0.01 to 0.14
- couple: float32 [3, 32, 64, 128], P(None, 'level', 'brick'), may hold values from 0.1 to 0.6
- solid: int32 [32, 64, 128], P('level', 'brick'), may hold values 0 or 1
- coarse_owner: int32 [4], replicated, may hold values from 0 to 3, each once
Outputs:
- smoothed: float32 [5, 32, 64, 128], P(None, 'level', 'brick')
- coarse_rhs: float32 [4, 5, 16, 32, 16], P('level', None, None, 'brick')
The draws below stay inside these ranges and needn't reach their ends.
Inputs may be any that keep to these rules, and one draw needn't show every extreme that they name: `coarse_owner`: each level index owns exactly one block.
All inputs are finite; a program needn't handle non-finite values. No bound on the sum of `solid` on one device may be relied on, other than what follows from the above.
Results may differ from the reference program's by a relative error of at most 0.0003.
Values may be sent and summed in bfloat16 or wider, within the bound.
A program may use at most 64 MiB of HBM per device.

```python
import jax
import jax.numpy as jnp
from jax import lax

FIELDS = 5
SWEEPS = 4
NX = 32
NY = 64
NZ = 128
N_LEVEL = 4


def diagonal_scale(key):
    return jax.random.uniform(jax.random.fold_in(key, 11), (NX, NY, NZ), jnp.float32, 8.0, 12.0)


def draw_block(key, part):
    scale_cells = diagonal_scale(key)
    spread = jax.random.uniform(jax.random.fold_in(key, 12), (FIELDS, FIELDS, NX, NY, NZ), jnp.float32, -0.06, 0.06)
    identity = jnp.eye(FIELDS, dtype=jnp.float32)[:, :, None, None, None]
    return (scale_cells * (identity + spread)).astype(jnp.bfloat16)


def draw_precond(key, part):
    scale_cells = diagonal_scale(key)
    spread = jax.random.uniform(jax.random.fold_in(key, 13), (FIELDS, FIELDS, NX, NY, NZ), jnp.float32, -0.06, 0.06)
    identity = jnp.eye(FIELDS, dtype=jnp.float32)[:, :, None, None, None]
    return ((identity + spread) / scale_cells).astype(jnp.bfloat16)


def set_ends(values, key, smallest, high):
    shape = values.shape
    spot = [jax.random.randint(jax.random.fold_in(key, axis), (), 0, shape[axis]) for axis in range(len(shape))]
    values = values.at[tuple(spot)].set(smallest)
    longest = shape.index(max(shape))
    spot[longest] = (spot[longest] + 1) % shape[longest]
    return values.at[tuple(spot)].set(high)


def level_of(stream_key, shape, cuts, low, largest):
    def one(position, blocks):
        steps = jax.random.uniform(jax.random.fold_in(jax.random.fold_in(stream_key, 6), position), (blocks,), jnp.float32, low / len(cuts), largest / len(cuts))
        return jnp.repeat(jnp.exp(steps), shape[position] // blocks).reshape((-1,) + (1,) * (len(shape) - position - 1))

    loudness = one(*cuts[0])
    for cut in cuts[1:]:
        loudness = loudness * one(*cut)
    return loudness


def bell_draw(rng, shape, scale, limit, shards=(), kind=jnp.bfloat16):
    entries = scale * jax.random.normal(rng, shape, jnp.float32)
    if shards:
        entries = entries * level_of(rng, shape, shards, -0.22, 0.18)
    return jnp.clip(entries, -limit, limit).astype(kind)


def setup_inputs(seed: int = 0) -> dict:
    key_of = jax.random.split(jax.random.key(seed), 8)
    adjoint = bell_draw(key_of[0], (FIELDS, NX, NY, NZ), 1.0, 6.0, ((1, 4), (2, 8)), jnp.float32)
    source = bell_draw(key_of[1], (FIELDS, NX, NY, NZ), 8.0, 48.0, ((1, 4), (2, 8)), jnp.float32)
    block = draw_block(jax.random.fold_in(key_of[7], 71), 0)
    precond = draw_precond(jax.random.fold_in(key_of[7], 71), 0)
    couple = jnp.clip(0.1 + 0.5 * jax.random.uniform(key_of[4], (3, NX, NY, NZ), jnp.float32) ** level_of(key_of[4], (3, NX, NY, NZ), ((1, 4), (2, 8)), -0.2, 0.2), 0.1, 0.6)
    solid = set_ends((jax.random.randint(key_of[5], (NX, NY, NZ), 0, 8) < 1).astype(jnp.int32), jax.random.fold_in(key_of[5], 1), 0, 1)
    coarse_owner = jax.random.permutation(key_of[6], N_LEVEL).astype(jnp.int32)
    return {"adjoint": adjoint, "source": source, "block": block, "precond": precond, "couple": couple, "solid": solid, "coarse_owner": coarse_owner}


relax_factor = 0.8


def apply_operator(padded, block, couple):
    center = padded[:, 1:-1, 1:-1, :]
    fields = []
    for outer in range(FIELDS):
        total = block[0, outer].astype(jnp.float32) * center[0]
        for inner in range(1, FIELDS):
            total = total + block[inner, outer].astype(jnp.float32) * center[inner]
        fields.append(total)
    diagonal_part = jnp.stack(fields)
    across_x = padded[:, 2:, 1:-1, :] + padded[:, :-2, 1:-1, :]
    across_y = padded[:, 1:-1, 2:, :] + padded[:, 1:-1, :-2, :]
    zero_plane = jnp.zeros_like(center[..., :1])
    across_z = jnp.concatenate([center[..., 1:], zero_plane], -1) + jnp.concatenate([zero_plane, center[..., :-1]], -1)
    coupled = couple[0] * across_x + couple[1] * across_y + couple[2] * across_z
    return diagonal_part - coupled


def precondition(precond, defect):
    fields = []
    for outer in range(FIELDS):
        total = precond[outer, 0].astype(jnp.float32) * defect[0]
        for inner in range(1, FIELDS):
            total = total + precond[outer, inner].astype(jnp.float32) * defect[inner]
        fields.append(total)
    return jnp.stack(fields)


def restrict_along(field, axis, before):
    length = field.shape[axis]
    even = lax.slice_in_dim(field, 0, length, 2, axis)
    odd = lax.slice_in_dim(field, 1, length, 2, axis)
    earlier = jnp.concatenate([before, lax.slice_in_dim(odd, 0, odd.shape[axis] - 1, 1, axis)], axis)
    return 0.5 * even + 0.25 * odd + 0.25 * earlier


def zero_first(field, axis):
    return jnp.zeros_like(lax.slice_in_dim(field, 0, 1, 1, axis))


def reference(adjoint, source, block, precond, couple, solid, coarse_owner):
    keep = solid == 0
    smoothed = adjoint
    for sweep in range(SWEEPS):
        padded = jnp.pad(smoothed, ((0, 0), (1, 1), (1, 1), (0, 0)))
        defect = source - apply_operator(padded, block, couple)
        smoothed = jnp.where(keep, smoothed + relax_factor * precondition(precond, defect), 0.0)
    padded = jnp.pad(smoothed, ((0, 0), (1, 1), (1, 1), (0, 0)))
    residual = jnp.where(keep, source - apply_operator(padded, block, couple), 0.0)
    coarse_z = restrict_along(residual, 3, zero_first(residual, 3))
    coarse_y = restrict_along(coarse_z, 2, zero_first(coarse_z, 2))
    coarse = restrict_along(coarse_y, 1, zero_first(coarse_y, 1))
    pieces = coarse.reshape(FIELDS, NX // 2, NY // 2, N_LEVEL, NZ // (2 * N_LEVEL)).transpose(3, 0, 1, 2, 4)
    coarse_rhs = jnp.zeros_like(pieces).at[coarse_owner].set(pieces)
    return smoothed, coarse_rhs
```

```python
import functools

import jax
import jax.numpy as jnp
from jax import lax
from jax.experimental import pallas as pl
from jax.experimental.pallas import tpu as pltpu
from jax.sharding import PartitionSpec as P

SWEEPS = 4
RELAX = 0.8
MESH = pl.DeviceIdType.MESH


def kernel(
    bricks, levels, fields, nx, ny, zblock,
    owner, adjoint, source, block, precond, couple, solid,
    smoothed, coarse,
    cells, src, raw_b, raw_p, mat_b, mat_p, cpl, sld, near, part, out_halo, in_halo,
    rows_x, packed, got, got_edge, merged,
    in_sem, out_sem, halo_send, halo_recv, end_send, end_recv,
):
    plane = nx * ny
    nz = cells.shape[1]
    half_x, half_y = nx // 2, ny // 2
    width = half_x + 1
    pad = rows_x.shape[0] // ny
    b, l = lax.axis_index("brick"), lax.axis_index("level")
    has = (l < levels - 1, l > 0, b < bricks - 1, b > 0)
    dest = ((b, l - 1), (b, l + 1), (b - 1, l), (b + 1, l))
    can_send = (has[1], has[0], has[3], has[2])

    loads = [
        pltpu.make_async_copy(a, v, in_sem.at[i])
        for i, (a, v) in enumerate(
            (
                (adjoint, cells), (couple, cpl), (block, raw_b),
                (source, src), (solid, sld), (precond, raw_p),
            )
        )
    ]
    for copy in loads:
        copy.start()

    barrier = pltpu.get_barrier_semaphore()
    for k in range(levels):
        to = lax.rem(l + k, levels)
        if k:
            pl.semaphore_signal(barrier, inc=1, device_id=(b, to), device_id_type=MESH)

        @pl.when(has[3])
        def _():
            pl.semaphore_signal(barrier, inc=1, device_id=(b - 1, to), device_id_type=MESH)

        @pl.when(has[2])
        def _():
            pl.semaphore_signal(barrier, inc=1, device_id=(b + 1, to), device_id_type=MESH)

    for i in range(4):

        @pl.when(jnp.logical_not(has[i]))
        def _():
            for e in range(SWEEPS + 1):
                in_halo[e, i] = jnp.zeros(in_halo.shape[2:], jnp.float32)

    @pl.when(jnp.logical_not(has[3]))
    def _():
        got_edge[...] = jnp.zeros_like(got_edge)

    def halo_copy(e, i):
        return pltpu.make_async_remote_copy(
            src_ref=out_halo.at[e, i],
            dst_ref=in_halo.at[e, i],
            send_sem=halo_send.at[e, i],
            recv_sem=halo_recv.at[e, i],
            device_id=dest[i],
            device_id_type=MESH,
        )

    def send(e):
        for f in range(fields):
            at, to = f * plane, f * nx
            out_halo[e, 2, to : to + nx] = cells[pl.ds(at, nx, stride=ny), :]
            out_halo[e, 3, to : to + nx] = cells[pl.ds(at + ny - 1, nx, stride=ny), :]
            to = f * ny
            out_halo[e, 0, to : to + ny] = cells[at : at + ny]
            out_halo[e, 1, to : to + ny] = cells[at + plane - ny : at + plane]
        for i in (2, 3, 0, 1):

            @pl.when(can_send[i])
            def _():
                halo_copy(e, i).start()

    loads[0].wait()
    neighbours = (levels - 1) + levels * (
        has[3].astype(jnp.int32) + has[2].astype(jnp.int32)
    )
    pl.semaphore_wait(barrier, neighbours)
    send(0)

    loads[1].wait()
    shape = (nx, ny, nz)
    row = lax.broadcasted_iota(jnp.int32, shape, 1).reshape(plane, nz)
    lane = lax.broadcasted_iota(jnp.int32, (plane, nz), 1)
    cy, cz = cpl[plane : 2 * plane], cpl[2 * plane :]
    near[0] = jnp.where(row == ny - 1, 0.0, cy)
    near[1] = jnp.where(row == 0, 0.0, cy)
    near[2] = jnp.where(lane == nz - 1, 0.0, cz)
    near[3] = jnp.where(lane == 0, 0.0, cz)
    loads[2].wait()
    for i in range(fields * fields):
        mat_b[i] = raw_b[i].astype(jnp.float32)
    loads[3].wait()

    def local_part(f):
        at = f * plane
        mid = cells[at : at + plane]
        cube = mid.reshape(shape)
        total = src[at : at + plane]
        for g in range(fields):
            total = total - mat_b[g * fields + f] * cells[g * plane : (g + 1) * plane]
        total = total + near[0] * pltpu.roll(cube, ny - 1, 1).reshape(plane, nz)
        total = total + near[1] * pltpu.roll(cube, 1, 1).reshape(plane, nz)
        total = total + near[2] * pltpu.roll(mid, nz - 1, 1)
        total = total + near[3] * pltpu.roll(mid, 1, 1)
        c = cpl[0:plane]
        part[at : at + ny] = total[:ny] + c[:ny] * mid[ny : 2 * ny]
        part[at + ny : at + plane - ny] = total[ny : plane - ny] + c[ny : plane - ny] * (
            mid[2 * ny :] + mid[: plane - 2 * ny]
        )
        part[at + plane - ny : at + plane] = (
            total[plane - ny :] + c[plane - ny :] * mid[plane - 2 * ny : plane - ny]
        )

    def arrive(e):
        for i in (2, 3, 0, 1):

            @pl.when(has[i])
            def _():
                halo_copy(e, i).wait_recv()

        low_y = cpl[pl.ds(plane, nx, stride=ny), :]
        high_y = cpl[pl.ds(plane + ny - 1, nx, stride=ny), :]
        low_x, high_x = cpl[0:ny], cpl[plane - ny : plane]
        for f in range(fields):
            at = f * plane
            mine = slice(f * ny, (f + 1) * ny)
            part[at + plane - ny : at + plane] += high_x * in_halo[e, 0, mine]
            part[at : at + ny] += low_x * in_halo[e, 1, mine]
            mine = slice(f * nx, (f + 1) * nx)
            spot = pl.ds(at + ny - 1, nx, stride=ny)
            part[spot, :] = part[spot, :] + high_y * in_halo[e, 2, mine]
            spot = pl.ds(at, nx, stride=ny)
            part[spot, :] = part[spot, :] + low_y * in_halo[e, 3, mine]

    for f in range(fields):
        local_part(f)
    loads[4].wait()
    loads[5].wait()
    keep = sld[...] == 0
    for i in range(fields * fields):
        mat_p[i] = jnp.where(keep, RELAX * raw_p[i].astype(jnp.float32), 0.0)

    for sweep in range(SWEEPS):
        if sweep:
            for f in range(fields):
                local_part(f)
        arrive(sweep)
        for f in range(fields):
            at = f * plane
            total = cells[at : at + plane]
            if sweep == 0:
                total = jnp.where(keep, total, 0.0)
            for g in range(fields):
                total = total + mat_p[f * fields + g] * part[g * plane : (g + 1) * plane]
            cells[at : at + plane] = total
        send(sweep + 1)

    store = pltpu.make_async_copy(cells, smoothed, out_sem)
    store.start()
    for f in range(fields):
        local_part(f)
    fine = lax.broadcasted_iota(jnp.int32, (nz, nz), 0)
    column = lax.broadcasted_iota(jnp.int32, (nz, nz), 1)
    target = column // zblock
    start_of = jnp.full((nz, nz), -nz, jnp.int32)
    for k in range(levels):
        start_of = jnp.where(target == owner[k], k * zblock, start_of)
    gap = fine - 2 * (start_of + column % zblock)
    weight = jnp.where(
        gap == 0, 0.5, jnp.where((gap == 1) | (gap == -1), 0.25, 0.0)
    ).astype(jnp.bfloat16)
    rows_x[...] = jnp.zeros_like(rows_x)
    arrive(SWEEPS)

    for f in range(fields):
        res = jnp.where(keep, part[f * plane : (f + 1) * plane], 0.0)
        cut = [res[x * ny : (x + 1) * ny] for x in range(nx)]
        for k in range(width):
            if k == half_x:
                value = 0.25 * cut[nx - 1]
            else:
                value = 0.5 * cut[2 * k] + 0.25 * cut[2 * k + 1]
                if k:
                    value = value + 0.25 * cut[2 * k - 1]
            spot = (f * width + k) * ny
            rows_x[spot : spot + ny] = value
    line = [rows_x[pl.ds(y, pad, stride=ny), :] for y in range(ny)]
    groups = []
    for k in range(half_y):
        value = 0.5 * line[2 * k] + 0.25 * line[2 * k + 1]
        if k:
            value = value + 0.25 * line[2 * k - 1]
        groups.append(value)
    groups.append(0.25 * line[ny - 1])
    stacked = jnp.concatenate(groups, 0)
    high = stacked.astype(jnp.bfloat16)
    low = (stacked - high.astype(jnp.float32)).astype(jnp.bfloat16)
    product = jnp.dot(high, weight, preferred_element_type=jnp.float32) + jnp.dot(
        low, weight, preferred_element_type=jnp.float32
    )
    spot_of = lax.broadcasted_iota(jnp.int32, (pad, nz), 1) // zblock
    for d in range(levels):
        total = jnp.zeros((pad, nz), jnp.float32)
        for k in range(half_y + 1):
            shift = ((k - d) * zblock) % nz
            moved = product[k * pad : (k + 1) * pad]
            if shift:
                moved = pltpu.roll(moved, shift, 1)
            total = jnp.where(spot_of == k, moved, total)
        packed[d] = total

    def end_copy(k, edge):
        to = lax.rem(l + k, levels)
        return pltpu.make_async_remote_copy(
            src_ref=packed.at[to],
            dst_ref=(got_edge if edge else got).at[l],
            send_sem=end_send.at[edge, k],
            recv_sem=end_recv.at[edge, k],
            device_id=(b + edge, to),
            device_id_type=MESH,
        )

    def end_arrival(k, edge):
        origin = lax.rem(l + levels - k, levels)
        return pltpu.make_async_remote_copy(
            src_ref=packed.at[l],
            dst_ref=(got_edge if edge else got).at[origin],
            send_sem=end_send.at[edge, k],
            recv_sem=end_recv.at[edge, k],
            device_id=(b, origin),
            device_id_type=MESH,
        )

    @pl.when(has[2])
    def _():
        for k in range(levels):
            end_copy(k, 1).start()

    for k in range(1, levels):
        end_copy(k, 0).start()
    got[l] = packed[l]
    store.wait()
    for e in range(SWEEPS + 1):
        for i in range(4):

            @pl.when(can_send[i])
            def _():
                halo_copy(e, i).wait_send()

    for k in range(1, levels):
        end_arrival(k, 0).wait_recv()

    @pl.when(has[3])
    def _():
        for k in range(levels):
            end_arrival(k, 1).wait_recv()

    for s in range(levels):
        edge = pltpu.roll(got_edge[s], (-half_y * zblock) % nz, 1)
        merged[s] = got[s] + jnp.where(spot_of == 0, edge, 0.0)
    for f in range(fields):
        for s in range(levels):
            at = f * width
            coarse[f, s * half_x : (s + 1) * half_x] = merged[s, at : at + half_x]
            if s:
                coarse[f, s * half_x : s * half_x + 1] = (
                    merged[s, at : at + 1] + merged[s - 1, at + half_x : at + width]
                )

    for k in range(1, levels):
        end_copy(k, 0).wait_send()

    @pl.when(has[2])
    def _():
        for k in range(levels):
            end_copy(k, 1).wait_send()


def shards(bricks, levels, adjoint, source, block, precond, couple, solid, coarse_owner):
    fields, nx, ny, nz = adjoint.shape
    plane = nx * ny
    zblock = nz // (2 * levels)
    half_x, half_y = nx // 2, ny // 2
    pad = -(-fields * (half_x + 1) // 8) * 8
    flat = fields * plane
    halo = fields * max(nx, ny)
    f32, bf16 = jnp.float32, jnp.bfloat16
    vmem, dma = pltpu.VMEM, pltpu.SemaphoreType.DMA
    anywhere = pl.BlockSpec(memory_space=pl.ANY)
    cells, coarse = pl.pallas_call(
        functools.partial(kernel, bricks, levels, fields, nx, ny, zblock),
        out_shape=(
            jax.ShapeDtypeStruct((flat, nz), f32),
            jax.ShapeDtypeStruct((fields, levels * half_x, nz), f32),
        ),
        in_specs=[pl.BlockSpec(memory_space=pltpu.SMEM)] + [anywhere] * 6,
        out_specs=(anywhere, pl.BlockSpec(memory_space=pltpu.VMEM)),
        scratch_shapes=[
            vmem((flat, nz), f32),
            vmem((flat, nz), f32),
            vmem((fields * fields, plane, nz), bf16),
            vmem((fields * fields, plane, nz), bf16),
            vmem((fields * fields, plane, nz), f32),
            vmem((fields * fields, plane, nz), f32),
            vmem((3 * plane, nz), f32),
            vmem((plane, nz), jnp.int32),
            vmem((4, plane, nz), f32),
            vmem((flat, nz), f32),
            vmem((SWEEPS + 1, 4, halo, nz), f32),
            vmem((SWEEPS + 1, 4, halo, nz), f32),
            vmem((pad * ny, nz), f32),
            vmem((levels, pad, nz), f32),
            vmem((levels, pad, nz), f32),
            vmem((levels, pad, nz), f32),
            vmem((levels, pad, nz), f32),
            dma((6,)),
            dma,
            dma((SWEEPS + 1, 4)),
            dma((SWEEPS + 1, 4)),
            dma((2, levels)),
            dma((2, levels)),
        ],
        compiler_params=pltpu.CompilerParams(
            collective_id=0, has_side_effects=True, vmem_limit_bytes=32 * 1024 * 1024
        ),
    )(
        coarse_owner,
        adjoint.reshape(flat, nz),
        source.reshape(flat, nz),
        block.reshape(fields * fields, plane, nz),
        precond.reshape(fields * fields, plane, nz),
        couple.reshape(3 * plane, nz),
        solid.reshape(plane, nz),
    )
    rhs = coarse[:, :, : half_y * zblock].reshape(
        1, fields, levels * half_x, half_y, zblock
    )
    return cells.reshape(adjoint.shape), rhs


def solution(mesh):
    cells = P(None, "level", "brick", None)
    blocks = P(None, None, "level", "brick", None)
    return jax.shard_map(
        functools.partial(shards, mesh.shape["brick"], mesh.shape["level"]),
        mesh=mesh,
        in_specs=(cells, cells, blocks, blocks, cells, P("level", "brick", None), P()),
        out_specs=(cells, P("level", None, None, "brick", None)),
        check_vma=False,
    )
```

```python
import functools

import jax
import jax.numpy as jnp
from jax import lax
from jax.experimental import pallas as pl
from jax.experimental.pallas import tpu as pltpu
from jax.sharding import PartitionSpec as P

SWEEPS = 4
RELAX = 0.8
MESH = pl.DeviceIdType.MESH


def kernel(
    bricks, levels, fields, nx, ny, zblock,
    owners, adjoint, source, block, precond, couple, solid,
    smoothed, coarse,
    owner, cells, src, raw_b, raw_p, mat_b, mat_p, cpl, sld, near, part, out_halo, in_halo,
    beyond, rows_x, rows_b, packed, got, got_edge, got_low, merged,
    in_sem, out_sem, halo_send, halo_recv, end_send, end_recv,
):
    plane = nx * ny
    nz = cells.shape[1]
    half_x, half_y = nx // 2, ny // 2
    width = half_x + 2
    halo = fields * max(nx, ny)
    pad = rows_x.shape[0] // ny
    b, l = lax.axis_index("brick"), lax.axis_index("level")
    has = (l < levels - 1, l > 0, b < bricks - 1, b > 0)
    dest = ((b, l - 1), (b, l + 1), (b - 1, l), (b + 1, l))
    can_send = (has[1], has[0], has[3], has[2])

    loads = [
        pltpu.make_async_copy(a, v, in_sem.at[i])
        for i, (a, v) in enumerate(
            (
                (adjoint, cells), (couple, cpl), (block, raw_b),
                (source, src), (solid, sld), (precond, raw_p), (owners, owner),
            )
        )
    ]
    for copy in loads:
        copy.start()

    barrier = pltpu.get_barrier_semaphore()
    for k in range(levels):
        to = lax.rem(l + k, levels)
        if k:
            pl.semaphore_signal(barrier, inc=1, device_id=(b, to), device_id_type=MESH)

        @pl.when(has[3])
        def _():
            pl.semaphore_signal(barrier, inc=1, device_id=(b - 1, to), device_id_type=MESH)

        @pl.when(has[2])
        def _():
            pl.semaphore_signal(barrier, inc=1, device_id=(b + 1, to), device_id_type=MESH)

    for i in range(4):

        @pl.when(jnp.logical_not(has[i]))
        def _():
            for e in range(SWEEPS):
                in_halo[e, i] = jnp.zeros(in_halo.shape[2:], jnp.float32)

    @pl.when(jnp.logical_not(has[3]))
    def _():
        got_edge[...] = jnp.zeros_like(got_edge)

    @pl.when(jnp.logical_not(has[2]))
    def _():
        got_low[...] = jnp.zeros_like(got_low)

    def halo_copy(e, i):
        rows = pl.ds(0, out_halo.shape[2] if e == 1 else halo)
        return pltpu.make_async_remote_copy(
            src_ref=out_halo.at[e, i, rows],
            dst_ref=in_halo.at[e, i, rows],
            send_sem=halo_send.at[e, i],
            recv_sem=halo_recv.at[e, i],
            device_id=dest[i],
            device_id_type=MESH,
        )

    def send(e):
        for f in range(fields):
            at, to = f * plane, f * nx
            out_halo[e, 2, to : to + nx] = cells[pl.ds(at, nx, stride=ny), :]
            out_halo[e, 3, to : to + nx] = cells[pl.ds(at + ny - 1, nx, stride=ny), :]
            to = f * ny
            out_halo[e, 0, to : to + ny] = cells[at : at + ny]
            out_halo[e, 1, to : to + ny] = cells[at + plane - ny : at + plane]
        if e == 1:
            edges = (
                (0, slice(0, ny), 0, ny),
                (1, slice(plane - ny, plane), 0, ny),
                (2, pl.ds(0, nx, stride=ny), plane, nx),
                (3, pl.ds(ny - 1, nx, stride=ny), plane, nx),
            )
            for i, spot, at, count in edges:
                if i < 2:
                    open_cells = sld[spot] == 0
                    weights = cpl[spot]
                else:
                    open_cells = sld[spot, :] == 0
                    weights = cpl[pl.ds(at + (ny - 1 if i == 3 else 0), nx, stride=ny), :]
                out_halo[e, i, halo : halo + count] = jnp.where(open_cells, weights, 0.0)
        for i in (2, 3, 0, 1):

            @pl.when(can_send[i])
            def _():
                halo_copy(e, i).start()

    loads[0].wait()
    neighbours = (levels - 1) + levels * (
        has[3].astype(jnp.int32) + has[2].astype(jnp.int32)
    )
    pl.semaphore_wait(barrier, neighbours)
    send(0)

    loads[1].wait()
    shape = (nx, ny, nz)
    row = lax.broadcasted_iota(jnp.int32, shape, 1).reshape(plane, nz)
    lane = lax.broadcasted_iota(jnp.int32, (plane, nz), 1)
    cy, cz = cpl[plane : 2 * plane], cpl[2 * plane :]
    near[0] = jnp.where(row == ny - 1, 0.0, cy)
    near[1] = jnp.where(row == 0, 0.0, cy)
    near[2] = jnp.where(lane == nz - 1, 0.0, cz)
    near[3] = jnp.where(lane == 0, 0.0, cz)
    loads[2].wait()
    for i in range(fields * fields):
        mat_b[i] = raw_b[i].astype(jnp.float32)
    loads[3].wait()

    def local_part(f):
        at = f * plane
        mid = cells[at : at + plane]
        cube = mid.reshape(shape)
        total = src[at : at + plane]
        for g in range(fields):
            total = total - mat_b[g * fields + f] * cells[g * plane : (g + 1) * plane]
        total = total + near[0] * pltpu.roll(cube, ny - 1, 1).reshape(plane, nz)
        total = total + near[1] * pltpu.roll(cube, 1, 1).reshape(plane, nz)
        total = total + near[2] * pltpu.roll(mid, nz - 1, 1)
        total = total + near[3] * pltpu.roll(mid, 1, 1)
        c = cpl[0:plane]
        part[at : at + ny] = total[:ny] + c[:ny] * mid[ny : 2 * ny]
        part[at + ny : at + plane - ny] = total[ny : plane - ny] + c[ny : plane - ny] * (
            mid[2 * ny :] + mid[: plane - 2 * ny]
        )
        part[at + plane - ny : at + plane] = (
            total[plane - ny :] + c[plane - ny :] * mid[plane - 2 * ny : plane - ny]
        )

    def arrive(e):
        for i in (2, 3, 0, 1):

            @pl.when(has[i])
            def _():
                halo_copy(e, i).wait_recv()

        low_y = cpl[pl.ds(plane, nx, stride=ny), :]
        high_y = cpl[pl.ds(plane + ny - 1, nx, stride=ny), :]
        low_x, high_x = cpl[0:ny], cpl[plane - ny : plane]
        for f in range(fields):
            at = f * plane
            mine = slice(f * ny, (f + 1) * ny)
            part[at + plane - ny : at + plane] += high_x * in_halo[e, 0, mine]
            part[at : at + ny] += low_x * in_halo[e, 1, mine]
            mine = slice(f * nx, (f + 1) * nx)
            spot = pl.ds(at + ny - 1, nx, stride=ny)
            part[spot, :] = part[spot, :] + high_y * in_halo[e, 2, mine]
            spot = pl.ds(at, nx, stride=ny)
            part[spot, :] = part[spot, :] + low_y * in_halo[e, 3, mine]

    for f in range(fields):
        local_part(f)
    loads[4].wait()
    loads[5].wait()
    loads[6].wait()
    keep = sld[...] == 0
    for i in range(fields * fields):
        mat_p[i] = jnp.where(keep, RELAX * raw_p[i].astype(jnp.float32), 0.0)

    for sweep in range(SWEEPS):
        if sweep:
            for f in range(fields):
                local_part(f)
        arrive(sweep)
        for f in range(fields):
            at = f * plane
            total = cells[at : at + plane]
            if sweep == 0:
                total = jnp.where(keep, total, 0.0)
            for g in range(fields):
                total = total + mat_p[f * fields + g] * part[g * plane : (g + 1) * plane]
            cells[at : at + plane] = total
        if sweep < SWEEPS - 1:
            send(sweep + 1)

    store = pltpu.make_async_copy(cells, smoothed, out_sem)
    store.start()
    for f in range(fields):
        local_part(f)
    fine = lax.broadcasted_iota(jnp.int32, (nz, nz), 0)
    column = lax.broadcasted_iota(jnp.int32, (nz, nz), 1)
    target = column // zblock
    start_of = jnp.full((nz, nz), -nz, jnp.int32)
    for k in range(levels):
        start_of = jnp.where(target == owner[k], k * zblock, start_of)
    gap = fine - 2 * (start_of + column % zblock)
    weight = jnp.where(
        gap == 0, 0.5, jnp.where((gap == 1) | (gap == -1), 0.25, 0.0)
    ).astype(jnp.bfloat16)
    rows_x[...] = jnp.zeros_like(rows_x)
    rows_b[...] = jnp.zeros_like(rows_b)
    beyond[...] = jnp.zeros_like(beyond)
    high_x, low_x = (in_halo[1, i, halo : halo + ny] for i in (0, 1))
    high_y, low_y = (in_halo[1, i, halo : halo + nx] for i in (2, 3))

    def restrict_x(target, f, cut):
        for k in range(-1, half_x + 1):
            value = 0.0
            for x, factor in ((2 * k - 1, 0.25), (2 * k, 0.5), (2 * k + 1, 0.25)):
                if x in cut:
                    value = value + factor * cut[x]
            if k >= 0 or -1 in cut:
                spot = (f * width + k + 1) * ny
                target[spot : spot + ny] = value

    for f in range(fields):
        res = jnp.where(keep, part[f * plane : (f + 1) * plane], 0.0)
        cut = {x: res[x * ny : (x + 1) * ny] for x in range(nx)}
        at = f * plane
        cut[-1] = low_x * cells[at : at + ny]
        cut[nx] = high_x * cells[at + plane - ny : at + plane]
        restrict_x(rows_x, f, cut)
        beyond[pl.ds(at, nx, stride=ny), :] = low_y * cells[pl.ds(at, nx, stride=ny), :]
        beyond[pl.ds(at + 1, nx, stride=ny), :] = (
            high_y * cells[pl.ds(at + ny - 1, nx, stride=ny), :]
        )
        restrict_x(
            rows_b, f, {x: beyond[at + x * ny : at + (x + 1) * ny] for x in range(nx)}
        )
    line = {y: rows_x[pl.ds(y, pad, stride=ny), :] for y in range(ny)}
    line[-1] = rows_b[pl.ds(0, pad, stride=ny), :]
    line[ny] = rows_b[pl.ds(1, pad, stride=ny), :]
    groups = []
    for k in [*range(half_y + 1), -1]:
        value = 0.0
        for y, factor in ((2 * k - 1, 0.25), (2 * k, 0.5), (2 * k + 1, 0.25)):
            if y in line:
                value = value + factor * line[y]
        groups.append(value)
    stacked = jnp.concatenate(groups, 0)
    high = stacked.astype(jnp.bfloat16)
    low = (stacked - high.astype(jnp.float32)).astype(jnp.bfloat16)
    product = jnp.dot(high, weight, preferred_element_type=jnp.float32) + jnp.dot(
        low, weight, preferred_element_type=jnp.float32
    )
    spot_of = lax.broadcasted_iota(jnp.int32, (pad, nz), 1) // zblock
    for d in range(levels):
        total = jnp.zeros((pad, nz), jnp.float32)
        for k in range(half_y + 2):
            shift = ((k - d) * zblock) % nz
            moved = product[k * pad : (k + 1) * pad]
            if shift:
                moved = pltpu.roll(moved, shift, 1)
            total = jnp.where(spot_of == k, moved, total)
        packed[d] = total

    def end_copy(k, edge):
        to = lax.rem(l + k, levels)
        return pltpu.make_async_remote_copy(
            src_ref=packed.at[to],
            dst_ref=(got, got_edge, got_low)[edge].at[l],
            send_sem=end_send.at[edge, k],
            recv_sem=end_recv.at[edge, k],
            device_id=(b + (0, 1, -1)[edge], to),
            device_id_type=MESH,
        )

    def end_arrival(k, edge):
        origin = lax.rem(l + levels - k, levels)
        return pltpu.make_async_remote_copy(
            src_ref=packed.at[l],
            dst_ref=(got, got_edge, got_low)[edge].at[origin],
            send_sem=end_send.at[edge, k],
            recv_sem=end_recv.at[edge, k],
            device_id=(b, origin),
            device_id_type=MESH,
        )

    @pl.when(has[2])
    def _():
        for k in range(levels):
            end_copy(k, 1).start()

    @pl.when(has[3])
    def _():
        for k in range(levels):
            end_copy(k, 2).start()

    for k in range(1, levels):
        end_copy(k, 0).start()
    got[l] = packed[l]
    store.wait()
    for e in range(SWEEPS):
        for i in range(4):

            @pl.when(can_send[i])
            def _():
                halo_copy(e, i).wait_send()

    for k in range(1, levels):
        end_arrival(k, 0).wait_recv()

    @pl.when(has[3])
    def _():
        for k in range(levels):
            end_arrival(k, 1).wait_recv()

    @pl.when(has[2])
    def _():
        for k in range(levels):
            end_arrival(k, 2).wait_recv()

    for s in range(levels):
        after = pltpu.roll(got_edge[s], (-half_y * zblock) % nz, 1)
        before = pltpu.roll(got_low[s], (-2 * zblock) % nz, 1)
        merged[s] = (
            got[s]
            + jnp.where(spot_of == 0, after, 0.0)
            + jnp.where(spot_of == half_y - 1, before, 0.0)
        )
    for f in range(fields):
        at = f * width
        for s in range(levels):
            to = s * half_x
            coarse[f, to : to + half_x] = merged[s, at + 1 : at + 1 + half_x]
        for s in range(1, levels):
            to = s * half_x
            coarse[f, to : to + 1] += merged[s - 1, at + width - 1 : at + width]
            coarse[f, to - 1 : to] += merged[s, at : at + 1]

    for k in range(1, levels):
        end_copy(k, 0).wait_send()

    @pl.when(has[2])
    def _():
        for k in range(levels):
            end_copy(k, 1).wait_send()

    @pl.when(has[3])
    def _():
        for k in range(levels):
            end_copy(k, 2).wait_send()


def shards(bricks, levels, adjoint, source, block, precond, couple, solid, coarse_owner):
    fields, nx, ny, nz = adjoint.shape
    plane = nx * ny
    zblock = nz // (2 * levels)
    half_x, half_y = nx // 2, ny // 2
    pad = -(-fields * (half_x + 2) // 8) * 8
    flat = fields * plane
    halo = fields * max(nx, ny)
    f32, bf16 = jnp.float32, jnp.bfloat16
    vmem, dma = pltpu.VMEM, pltpu.SemaphoreType.DMA
    anywhere = pl.BlockSpec(memory_space=pltpu.HBM)
    cells, coarse = pl.pallas_call(
        functools.partial(kernel, bricks, levels, fields, nx, ny, zblock),
        out_shape=(
            jax.ShapeDtypeStruct((flat, nz), f32),
            jax.ShapeDtypeStruct((fields, levels * half_x, nz), f32),
        ),
        in_specs=[anywhere] * 7,
        out_specs=(anywhere, pl.BlockSpec(memory_space=pltpu.VMEM)),
        scratch_shapes=[
            pltpu.SMEM((levels,), jnp.int32),
            vmem((flat, nz), f32),
            vmem((flat, nz), f32),
            vmem((fields * fields, plane, nz), bf16),
            vmem((fields * fields, plane, nz), bf16),
            vmem((fields * fields, plane, nz), f32),
            vmem((fields * fields, plane, nz), f32),
            vmem((3 * plane, nz), f32),
            vmem((plane, nz), jnp.int32),
            vmem((4, plane, nz), f32),
            vmem((flat, nz), f32),
            vmem((SWEEPS, 4, halo + max(nx, ny), nz), f32),
            vmem((SWEEPS, 4, halo + max(nx, ny), nz), f32),
            vmem((flat, nz), f32),
            vmem((pad * ny, nz), f32),
            vmem((pad * ny, nz), f32),
            vmem((levels, pad, nz), f32),
            vmem((levels, pad, nz), f32),
            vmem((levels, pad, nz), f32),
            vmem((levels, pad, nz), f32),
            vmem((levels, pad, nz), f32),
            dma((7,)),
            dma,
            dma((SWEEPS, 4)),
            dma((SWEEPS, 4)),
            dma((3, levels)),
            dma((3, levels)),
        ],
        compiler_params=pltpu.CompilerParams(
            collective_id=0, has_side_effects=True, vmem_limit_bytes=60 * 1024 * 1024
        ),
    )(
        coarse_owner,
        adjoint.reshape(flat, nz),
        source.reshape(flat, nz),
        block.reshape(fields * fields, plane, nz),
        precond.reshape(fields * fields, plane, nz),
        couple.reshape(3 * plane, nz),
        solid.reshape(plane, nz),
    )
    rhs = coarse[:, :, : half_y * zblock].reshape(
        1, fields, levels * half_x, half_y, zblock
    )
    return cells.reshape(adjoint.shape), rhs


def solution(mesh):
    cells = P(None, "level", "brick", None)
    blocks = P(None, None, "level", "brick", None)
    return jax.shard_map(
        functools.partial(shards, mesh.shape["brick"], mesh.shape["level"]),
        mesh=mesh,
        in_specs=(cells, cells, blocks, blocks, cells, P("level", "brick", None), P()),
        out_specs=(cells, P("level", None, None, "brick", None)),
        check_vma=False,
    )
```

```python
import functools

import jax
import jax.numpy as jnp
from jax import lax
from jax.experimental import pallas as pl
from jax.experimental.pallas import tpu as pltpu
from jax.sharding import PartitionSpec as P

SWEEPS = 4
RELAX = 0.8
MESH = pl.DeviceIdType.MESH


def kernel(
    bricks, levels, fields, nx, ny, zblock,
    owners, adjoint, source, block, precond, couple, solid,
    smoothed, coarse,
    owner, cells, src, raw_b, raw_p, mat_b, mat_p, cpl, sld, near, part, out_halo, in_halo,
    beyond, rows_x, rows_b, packed, packed_edge, sides, got, got_edge, got_low, merged,
    in_sem, out_sem, halo_send, halo_recv, end_send, end_recv,
):
    plane = nx * ny
    nz = cells.shape[1]
    half_x, half_y = nx // 2, ny // 2
    width = half_x + 2
    halo = fields * max(nx, ny)
    pad = rows_x.shape[0] // ny
    b, l = lax.axis_index("brick"), lax.axis_index("level")
    has = (l < levels - 1, l > 0, b < bricks - 1, b > 0)
    dest = ((b, l - 1), (b, l + 1), (b - 1, l), (b + 1, l))
    can_send = (has[1], has[0], has[3], has[2])

    loads = [
        pltpu.make_async_copy(a, v, in_sem.at[i])
        for i, (a, v) in enumerate(
            (
                (adjoint, cells), (couple, cpl), (block, raw_b),
                (source, src), (solid, sld), (precond, raw_p), (owners, owner),
            )
        )
    ]
    for copy in loads:
        copy.start()

    barrier = pltpu.get_barrier_semaphore()
    for k in range(levels):
        to = lax.rem(l + k, levels)
        if k:
            pl.semaphore_signal(barrier, inc=1, device_id=(b, to), device_id_type=MESH)

        @pl.when(has[3])
        def _():
            pl.semaphore_signal(barrier, inc=1, device_id=(b - 1, to), device_id_type=MESH)

        @pl.when(has[2])
        def _():
            pl.semaphore_signal(barrier, inc=1, device_id=(b + 1, to), device_id_type=MESH)

    for i in range(4):

        @pl.when(jnp.logical_not(has[i]))
        def _():
            for e in range(SWEEPS):
                in_halo[e, i] = jnp.zeros(in_halo.shape[2:], jnp.float32)

    @pl.when(jnp.logical_not(has[3]))
    def _():
        got_edge[...] = jnp.zeros_like(got_edge)

    @pl.when(jnp.logical_not(has[2]))
    def _():
        got_low[...] = jnp.zeros_like(got_low)

    def halo_copy(e, i):
        rows = pl.ds(0, out_halo.shape[2] if e == 1 else halo)
        return pltpu.make_async_remote_copy(
            src_ref=out_halo.at[e, i, rows],
            dst_ref=in_halo.at[e, i, rows],
            send_sem=halo_send.at[e, i],
            recv_sem=halo_recv.at[e, i],
            device_id=dest[i],
            device_id_type=MESH,
        )

    def start(e, i):
        @pl.when(can_send[i])
        def _():
            halo_copy(e, i).start()

    def send(e):
        if e == 1:
            edges = (
                (0, slice(0, ny), 0, ny),
                (1, slice(plane - ny, plane), 0, ny),
                (2, pl.ds(0, nx, stride=ny), plane, nx),
                (3, pl.ds(ny - 1, nx, stride=ny), plane, nx),
            )
            for i, spot, at, count in edges:
                if i < 2:
                    open_cells = sld[spot] == 0
                    weights = cpl[spot]
                else:
                    open_cells = sld[spot, :] == 0
                    weights = cpl[pl.ds(at + (ny - 1 if i == 3 else 0), nx, stride=ny), :]
                out_halo[e, i, halo : halo + count] = jnp.where(open_cells, weights, 0.0)
        if e == 0:
            for f in range(fields):
                at, to = f * plane, f * nx
                out_halo[e, 2, to : to + nx] = cells[pl.ds(at, nx, stride=ny), :]
                out_halo[e, 3, to : to + nx] = cells[pl.ds(at + ny - 1, nx, stride=ny), :]
        start(e, 2)
        start(e, 3)
        for f in range(fields):
            at, to = f * plane, f * ny
            out_halo[e, 0, to : to + ny] = cells[at : at + ny]
            out_halo[e, 1, to : to + ny] = cells[at + plane - ny : at + plane]
        start(e, 0)
        start(e, 1)

    loads[0].wait()
    neighbours = (levels - 1) + levels * (
        has[3].astype(jnp.int32) + has[2].astype(jnp.int32)
    )
    pl.semaphore_wait(barrier, neighbours)
    send(0)

    loads[1].wait()
    shape = (nx, ny, nz)
    row = lax.broadcasted_iota(jnp.int32, shape, 1).reshape(plane, nz)
    lane = lax.broadcasted_iota(jnp.int32, (plane, nz), 1)
    cy, cz = cpl[plane : 2 * plane], cpl[2 * plane :]
    near[0] = jnp.where(row == ny - 1, 0.0, cy)
    near[1] = jnp.where(row == 0, 0.0, cy)
    near[2] = jnp.where(lane == nz - 1, 0.0, cz)
    near[3] = jnp.where(lane == 0, 0.0, cz)
    loads[2].wait()
    for i in range(fields * fields):
        mat_b[i] = raw_b[i].astype(jnp.float32)
    loads[3].wait()

    def local_part(f):
        at = f * plane
        mid = cells[at : at + plane]
        cube = mid.reshape(shape)
        total = src[at : at + plane]
        for g in range(fields):
            total = total - mat_b[g * fields + f] * cells[g * plane : (g + 1) * plane]
        total = total + near[0] * pltpu.roll(cube, ny - 1, 1).reshape(plane, nz)
        total = total + near[1] * pltpu.roll(cube, 1, 1).reshape(plane, nz)
        total = total + near[2] * pltpu.roll(mid, nz - 1, 1)
        total = total + near[3] * pltpu.roll(mid, 1, 1)
        c = cpl[0:plane]
        part[at : at + ny] = total[:ny] + c[:ny] * mid[ny : 2 * ny]
        part[at + ny : at + plane - ny] = total[ny : plane - ny] + c[ny : plane - ny] * (
            mid[2 * ny :] + mid[: plane - 2 * ny]
        )
        part[at + plane - ny : at + plane] = (
            total[plane - ny :] + c[plane - ny :] * mid[plane - 2 * ny : plane - ny]
        )

    def arrive(e, i):
        @pl.when(has[i])
        def _():
            halo_copy(e, i).wait_recv()

    def add_x(e):
        arrive(e, 0)
        arrive(e, 1)
        for f in range(fields):
            at = f * plane
            mine = slice(f * ny, (f + 1) * ny)
            spot = slice(at + plane - ny, at + plane)
            part[spot] += cpl[plane - ny : plane] * in_halo[e, 0, mine]
            part[at : at + ny] += cpl[0:ny] * in_halo[e, 1, mine]

    def add_y(e):
        for i in (2, 3):
            arrive(e, i)
            row_at = ny - 1 if i == 2 else 0
            weights = cpl[pl.ds(plane + row_at, nx, stride=ny), :]
            change = [
                weights * in_halo[e, i, g * nx : (g + 1) * nx] for g in range(fields)
            ]
            for f in range(fields):
                spot = pl.ds(f * plane + row_at, nx, stride=ny)
                total = cells[spot, :]
                for g in range(fields):
                    total = total + sides[i - 2, f * fields + g] * change[g]
                cells[spot, :] = total
                if e < SWEEPS - 1:
                    out_halo[e + 1, 5 - i, f * nx : (f + 1) * nx] = total

    for f in range(fields):
        local_part(f)
    loads[4].wait()
    loads[5].wait()
    loads[6].wait()
    keep = sld[...] == 0
    for i in range(fields * fields):
        mat_p[i] = jnp.where(keep, RELAX * raw_p[i].astype(jnp.float32), 0.0)
        sides[0, i] = mat_p[i, pl.ds(ny - 1, nx, stride=ny), :]
        sides[1, i] = mat_p[i, pl.ds(0, nx, stride=ny), :]

    for sweep in range(SWEEPS):
        if sweep:
            for f in range(fields):
                local_part(f)
        add_x(sweep)
        for f in range(fields):
            at = f * plane
            total = cells[at : at + plane]
            if sweep == 0:
                total = jnp.where(keep, total, 0.0)
            for g in range(fields):
                total = total + mat_p[f * fields + g] * part[g * plane : (g + 1) * plane]
            cells[at : at + plane] = total
        add_y(sweep)
        if sweep < SWEEPS - 1:
            send(sweep + 1)

    store = pltpu.make_async_copy(cells, smoothed, out_sem)
    store.start()
    for f in range(fields):
        local_part(f)
    fine = lax.broadcasted_iota(jnp.int32, (nz, nz), 0)
    column = lax.broadcasted_iota(jnp.int32, (nz, nz), 1)
    target = column // zblock
    start_of = jnp.full((nz, nz), -nz, jnp.int32)
    for k in range(levels):
        start_of = jnp.where(target == owner[k], k * zblock, start_of)
    gap = fine - 2 * (start_of + column % zblock)
    weight = jnp.where(
        gap == 0, 0.5, jnp.where((gap == 1) | (gap == -1), 0.25, 0.0)
    ).astype(jnp.bfloat16)
    rows_x[...] = jnp.zeros_like(rows_x)
    rows_b[...] = jnp.zeros_like(rows_b)
    beyond[...] = jnp.zeros_like(beyond)
    high_x, low_x = (in_halo[1, i, halo : halo + ny] for i in (0, 1))
    high_y, low_y = (in_halo[1, i, halo : halo + nx] for i in (2, 3))

    def restrict_x(target, f, cut):
        for k in range(-1, half_x + 1):
            value = 0.0
            for x, factor in ((2 * k - 1, 0.25), (2 * k, 0.5), (2 * k + 1, 0.25)):
                if x in cut:
                    value = value + factor * cut[x]
            if k >= 0 or -1 in cut:
                spot = (f * width + k + 1) * ny
                target[spot : spot + ny] = value

    for f in range(fields):
        res = jnp.where(keep, part[f * plane : (f + 1) * plane], 0.0)
        cut = {x: res[x * ny : (x + 1) * ny] for x in range(nx)}
        at = f * plane
        cut[-1] = low_x * cells[at : at + ny]
        cut[nx] = high_x * cells[at + plane - ny : at + plane]
        restrict_x(rows_x, f, cut)
        beyond[pl.ds(at, nx, stride=ny), :] = low_y * cells[pl.ds(at, nx, stride=ny), :]
        beyond[pl.ds(at + 1, nx, stride=ny), :] = (
            high_y * cells[pl.ds(at + ny - 1, nx, stride=ny), :]
        )
        restrict_x(
            rows_b, f, {x: beyond[at + x * ny : at + (x + 1) * ny] for x in range(nx)}
        )
    line = {y: rows_x[pl.ds(y, pad, stride=ny), :] for y in range(ny)}
    line[-1] = rows_b[pl.ds(0, pad, stride=ny), :]
    line[ny] = rows_b[pl.ds(1, pad, stride=ny), :]
    groups = []
    for k in [*range(half_y + 1), -1]:
        value = 0.0
        for y, factor in ((2 * k - 1, 0.25), (2 * k, 0.5), (2 * k + 1, 0.25)):
            if y in line:
                value = value + factor * line[y]
        groups.append(value)
    stacked = jnp.concatenate(groups, 0)
    high = stacked.astype(jnp.bfloat16)
    low = (stacked - high.astype(jnp.float32)).astype(jnp.bfloat16)
    product = jnp.dot(high, weight, preferred_element_type=jnp.float32) + jnp.dot(
        low, weight, preferred_element_type=jnp.float32
    )
    spot_of = lax.broadcasted_iota(jnp.int32, (pad, nz), 1) // zblock
    for d in range(levels):
        total = jnp.zeros((pad, nz), jnp.float32)
        for k in range(half_y):
            shift = ((k - d) * zblock) % nz
            moved = product[k * pad : (k + 1) * pad]
            if shift:
                moved = pltpu.roll(moved, shift, 1)
            total = jnp.where(spot_of == k, moved, total)
        packed[d] = total
        for side in range(2):
            total = jnp.zeros((8, nz), jnp.float32)
            for k in range(pad // 8):
                at = (half_y + side) * pad + k * 8
                moved = product[at : at + 8]
                shift = ((k - d) * zblock) % nz
                if shift:
                    moved = pltpu.roll(moved, shift, 1)
                total = jnp.where(spot_of[:8] == k, moved, total)
            packed_edge[side, d] = total

    def end_copy(k, edge):
        to = lax.rem(l + k, levels)
        return pltpu.make_async_remote_copy(
            src_ref=packed_edge.at[edge - 1, to] if edge else packed.at[to],
            dst_ref=(got, got_edge, got_low)[edge].at[l],
            send_sem=end_send.at[edge, k],
            recv_sem=end_recv.at[edge, k],
            device_id=(b + (0, 1, -1)[edge], to),
            device_id_type=MESH,
        )

    def end_arrival(k, edge):
        origin = lax.rem(l + levels - k, levels)
        return pltpu.make_async_remote_copy(
            src_ref=packed_edge.at[edge - 1, l] if edge else packed.at[l],
            dst_ref=(got, got_edge, got_low)[edge].at[origin],
            send_sem=end_send.at[edge, k],
            recv_sem=end_recv.at[edge, k],
            device_id=(b, origin),
            device_id_type=MESH,
        )

    @pl.when(has[2])
    def _():
        for k in range(levels):
            end_copy(k, 1).start()

    @pl.when(has[3])
    def _():
        for k in range(levels):
            end_copy(k, 2).start()

    for k in range(1, levels):
        end_copy(k, 0).start()
    got[l] = packed[l]
    store.wait()
    for e in range(SWEEPS):
        for i in range(4):

            @pl.when(can_send[i])
            def _():
                halo_copy(e, i).wait_send()

    for k in range(1, levels):
        end_arrival(k, 0).wait_recv()

    @pl.when(has[3])
    def _():
        for k in range(levels):
            end_arrival(k, 1).wait_recv()

    @pl.when(has[2])
    def _():
        for k in range(levels):
            end_arrival(k, 2).wait_recv()

    for s in range(levels):
        for k in range(pad // 8):
            first = pltpu.roll(got_edge[s], (-k * zblock) % nz, 1)
            last = pltpu.roll(got_low[s], ((half_y - 1 - k) * zblock) % nz, 1)
            mine = slice(k * 8, k * 8 + 8)
            merged[s, mine] = (
                got[s, mine]
                + jnp.where(spot_of[:8] == 0, first, 0.0)
                + jnp.where(spot_of[:8] == half_y - 1, last, 0.0)
            )
    for f in range(fields):
        at = f * width
        for s in range(levels):
            to = s * half_x
            coarse[f, to : to + half_x] = merged[s, at + 1 : at + 1 + half_x]
        for s in range(1, levels):
            to = s * half_x
            coarse[f, to : to + 1] += merged[s - 1, at + width - 1 : at + width]
            coarse[f, to - 1 : to] += merged[s, at : at + 1]

    for k in range(1, levels):
        end_copy(k, 0).wait_send()

    @pl.when(has[2])
    def _():
        for k in range(levels):
            end_copy(k, 1).wait_send()

    @pl.when(has[3])
    def _():
        for k in range(levels):
            end_copy(k, 2).wait_send()


def shards(bricks, levels, adjoint, source, block, precond, couple, solid, coarse_owner):
    fields, nx, ny, nz = adjoint.shape
    plane = nx * ny
    zblock = nz // (2 * levels)
    half_x, half_y = nx // 2, ny // 2
    pad = -(-fields * (half_x + 2) // 8) * 8
    flat = fields * plane
    halo = fields * max(nx, ny)
    f32, bf16 = jnp.float32, jnp.bfloat16
    vmem, dma = pltpu.VMEM, pltpu.SemaphoreType.DMA
    anywhere = pl.BlockSpec(memory_space=pltpu.HBM)
    cells, coarse = pl.pallas_call(
        functools.partial(kernel, bricks, levels, fields, nx, ny, zblock),
        out_shape=(
            jax.ShapeDtypeStruct((flat, nz), f32),
            jax.ShapeDtypeStruct((fields, levels * half_x, nz), f32),
        ),
        in_specs=[anywhere] * 7,
        out_specs=(anywhere, pl.BlockSpec(memory_space=pltpu.VMEM)),
        scratch_shapes=[
            pltpu.SMEM((levels,), jnp.int32),
            vmem((flat, nz), f32),
            vmem((flat, nz), f32),
            vmem((fields * fields, plane, nz), bf16),
            vmem((fields * fields, plane, nz), bf16),
            vmem((fields * fields, plane, nz), f32),
            vmem((fields * fields, plane, nz), f32),
            vmem((3 * plane, nz), f32),
            vmem((plane, nz), jnp.int32),
            vmem((4, plane, nz), f32),
            vmem((flat, nz), f32),
            vmem((SWEEPS, 4, halo + max(nx, ny), nz), f32),
            vmem((SWEEPS, 4, halo + max(nx, ny), nz), f32),
            vmem((flat, nz), f32),
            vmem((pad * ny, nz), f32),
            vmem((pad * ny, nz), f32),
            vmem((levels, pad, nz), f32),
            vmem((2, levels, 8, nz), f32),
            vmem((2, fields * fields, nx, nz), f32),
            vmem((levels, pad, nz), f32),
            vmem((levels, 8, nz), f32),
            vmem((levels, 8, nz), f32),
            vmem((levels, pad, nz), f32),
            dma((7,)),
            dma,
            dma((SWEEPS, 4)),
            dma((SWEEPS, 4)),
            dma((3, levels)),
            dma((3, levels)),
        ],
        compiler_params=pltpu.CompilerParams(
            collective_id=0, has_side_effects=True, vmem_limit_bytes=60 * 1024 * 1024
        ),
    )(
        coarse_owner,
        adjoint.reshape(flat, nz),
        source.reshape(flat, nz),
        block.reshape(fields * fields, plane, nz),
        precond.reshape(fields * fields, plane, nz),
        couple.reshape(3 * plane, nz),
        solid.reshape(plane, nz),
    )
    rhs = coarse[:, :, : half_y * zblock].reshape(
        1, fields, levels * half_x, half_y, zblock
    )
    return cells.reshape(adjoint.shape), rhs


def solution(mesh):
    cells = P(None, "level", "brick", None)
    blocks = P(None, None, "level", "brick", None)
    return jax.shard_map(
        functools.partial(shards, mesh.shape["brick"], mesh.shape["level"]),
        mesh=mesh,
        in_specs=(cells, cells, blocks, blocks, cells, P("level", "brick", None), P()),
        out_specs=(cells, P("level", None, None, "brick", None)),
        check_vma=False,
    )
```

```python
import functools

import jax
import jax.numpy as jnp
from jax import lax
from jax.experimental import pallas as pl
from jax.experimental.pallas import tpu as pltpu
from jax.sharding import PartitionSpec as P

SWEEPS = 4
RELAX = 0.8
MESH = pl.DeviceIdType.MESH


def kernel(
    bricks, levels, fields, nx, ny, zblock,
    owners, adjoint, source, block, precond, couple, solid,
    smoothed, coarse,
    owner, cells, src, raw_b, raw_p, mat_b, mat_p, cpl, sld, near, part, out_halo, in_halo,
    beyond, rows_x, rows_b, packed, packed_edge, sides, got, got_edge, got_low, merged,
    in_sem, out_sem, halo_send, halo_recv, end_send, end_recv,
):
    plane = nx * ny
    nz = cells.shape[1]
    half_x, half_y = nx // 2, ny // 2
    width = half_x + 2
    halo = fields * max(nx, ny)
    pad = rows_x.shape[0] // ny
    b, l = lax.axis_index("brick"), lax.axis_index("level")
    has = (l < levels - 1, l > 0, b < bricks - 1, b > 0)
    dest = ((b, l - 1), (b, l + 1), (b - 1, l), (b + 1, l))
    can_send = (has[1], has[0], has[3], has[2])

    loads = [
        pltpu.make_async_copy(a, v, in_sem.at[i])
        for i, (a, v) in enumerate(
            (
                (adjoint, cells), (couple, cpl), (block, raw_b),
                (source, src), (solid, sld), (precond, raw_p), (owners, owner),
            )
        )
    ]
    for copy in loads:
        copy.start()

    barrier = pltpu.get_barrier_semaphore()
    for k in range(levels):
        to = lax.rem(l + k, levels)
        if k:
            pl.semaphore_signal(barrier, inc=1, device_id=(b, to), device_id_type=MESH)

        @pl.when(has[3])
        def _():
            pl.semaphore_signal(barrier, inc=1, device_id=(b - 1, to), device_id_type=MESH)

        @pl.when(has[2])
        def _():
            pl.semaphore_signal(barrier, inc=1, device_id=(b + 1, to), device_id_type=MESH)

    for i in range(4):

        @pl.when(jnp.logical_not(has[i]))
        def _():
            for e in range(SWEEPS):
                in_halo[e, i] = jnp.zeros(in_halo.shape[2:], jnp.float32)

    @pl.when(jnp.logical_not(has[3]))
    def _():
        got_edge[...] = jnp.zeros_like(got_edge)

    @pl.when(jnp.logical_not(has[2]))
    def _():
        got_low[...] = jnp.zeros_like(got_low)

    def halo_copy(e, i):
        rows = pl.ds(0, out_halo.shape[2] if e == 1 else halo)
        return pltpu.make_async_remote_copy(
            src_ref=out_halo.at[e, i, rows],
            dst_ref=in_halo.at[e, i, rows],
            send_sem=halo_send.at[e, i],
            recv_sem=halo_recv.at[e, i],
            device_id=dest[i],
            device_id_type=MESH,
        )

    def start(e, i):
        @pl.when(can_send[i])
        def _():
            halo_copy(e, i).start()

    def send(e):
        if e == 1:
            edges = (
                (0, slice(0, ny), 0, ny),
                (1, slice(plane - ny, plane), 0, ny),
                (2, pl.ds(0, nx, stride=ny), plane, nx),
                (3, pl.ds(ny - 1, nx, stride=ny), plane, nx),
            )
            for i, spot, at, count in edges:
                if i < 2:
                    open_cells = sld[spot] == 0
                    weights = cpl[spot]
                else:
                    open_cells = sld[spot, :] == 0
                    weights = cpl[pl.ds(at + (ny - 1 if i == 3 else 0), nx, stride=ny), :]
                out_halo[e, i, halo : halo + count] = jnp.where(open_cells, weights, 0.0)
        if e == 0:
            for f in range(fields):
                at, to = f * plane, f * nx
                out_halo[e, 2, to : to + nx] = cells[pl.ds(at, nx, stride=ny), :]
                out_halo[e, 3, to : to + nx] = cells[pl.ds(at + ny - 1, nx, stride=ny), :]
        start(e, 2)
        start(e, 3)
        for f in range(fields):
            at, to = f * plane, f * ny
            out_halo[e, 0, to : to + ny] = cells[at : at + ny]
            out_halo[e, 1, to : to + ny] = cells[at + plane - ny : at + plane]
        start(e, 0)
        start(e, 1)

    loads[0].wait()
    neighbours = (levels - 1) + levels * (
        has[3].astype(jnp.int32) + has[2].astype(jnp.int32)
    )
    pl.semaphore_wait(barrier, neighbours)
    send(0)

    loads[1].wait()
    shape = (nx, ny, nz)
    row = lax.broadcasted_iota(jnp.int32, shape, 1).reshape(plane, nz)
    lane = lax.broadcasted_iota(jnp.int32, (plane, nz), 1)
    cy, cz = cpl[plane : 2 * plane], cpl[2 * plane :]
    near[0] = jnp.where(row == ny - 1, 0.0, cy)
    near[1] = jnp.where(row == 0, 0.0, cy)
    near[2] = jnp.where(lane == nz - 1, 0.0, cz)
    near[3] = jnp.where(lane == 0, 0.0, cz)
    loads[2].wait()
    for i in range(fields * fields):
        mat_b[i] = raw_b[i].astype(jnp.float32)
    loads[3].wait()

    def local_part(f):
        at = f * plane
        mid = cells[at : at + plane]
        cube = mid.reshape(shape)
        total = src[at : at + plane]
        for g in range(fields):
            total = total - mat_b[g * fields + f] * cells[g * plane : (g + 1) * plane]
        total = total + near[0] * pltpu.roll(cube, ny - 1, 1).reshape(plane, nz)
        total = total + near[1] * pltpu.roll(cube, 1, 1).reshape(plane, nz)
        total = total + near[2] * pltpu.roll(mid, nz - 1, 1)
        total = total + near[3] * pltpu.roll(mid, 1, 1)
        c = cpl[0:plane]
        part[at : at + ny] = total[:ny] + c[:ny] * mid[ny : 2 * ny]
        part[at + ny : at + plane - ny] = total[ny : plane - ny] + c[ny : plane - ny] * (
            mid[2 * ny :] + mid[: plane - 2 * ny]
        )
        part[at + plane - ny : at + plane] = (
            total[plane - ny :] + c[plane - ny :] * mid[plane - 2 * ny : plane - ny]
        )

    def arrive(e, i):
        @pl.when(has[i])
        def _():
            halo_copy(e, i).wait_recv()

    def add_x(e):
        arrive(e, 0)
        arrive(e, 1)
        for f in range(fields):
            at = f * plane
            mine = slice(f * ny, (f + 1) * ny)
            spot = slice(at + plane - ny, at + plane)
            part[spot] += cpl[plane - ny : plane] * in_halo[e, 0, mine]
            part[at : at + ny] += cpl[0:ny] * in_halo[e, 1, mine]

    def add_y(e):
        for i in (2, 3):
            arrive(e, i)
            row_at = ny - 1 if i == 2 else 0
            weights = cpl[pl.ds(plane + row_at, nx, stride=ny), :]
            change = [
                weights * in_halo[e, i, g * nx : (g + 1) * nx] for g in range(fields)
            ]
            for f in range(fields):
                spot = pl.ds(f * plane + row_at, nx, stride=ny)
                total = cells[spot, :]
                for g in range(fields):
                    total = total + sides[i - 2, f * fields + g] * change[g]
                cells[spot, :] = total
                if e < SWEEPS - 1:
                    out_halo[e + 1, 5 - i, f * nx : (f + 1) * nx] = total

    for f in range(fields):
        local_part(f)
    loads[4].wait()
    loads[5].wait()
    loads[6].wait()
    keep = sld[...] == 0
    for i in range(fields * fields):
        mat_p[i] = jnp.where(keep, RELAX * raw_p[i].astype(jnp.float32), 0.0)
        sides[0, i] = mat_p[i, pl.ds(ny - 1, nx, stride=ny), :]
        sides[1, i] = mat_p[i, pl.ds(0, nx, stride=ny), :]

    for sweep in range(SWEEPS):
        if sweep:
            for f in range(fields):
                local_part(f)
        add_x(sweep)
        for f in range(fields):
            at = f * plane
            total = cells[at : at + plane]
            if sweep == 0:
                total = jnp.where(keep, total, 0.0)
            for g in range(fields):
                total = total + mat_p[f * fields + g] * part[g * plane : (g + 1) * plane]
            cells[at : at + plane] = total
        add_y(sweep)
        if sweep < SWEEPS - 1:
            send(sweep + 1)

    store = pltpu.make_async_copy(cells, smoothed, out_sem)
    store.start()
    for f in range(fields):
        local_part(f)
    fine = lax.broadcasted_iota(jnp.int32, (nz, nz), 0)
    column = lax.broadcasted_iota(jnp.int32, (nz, nz), 1)
    target = column // zblock
    start_of = jnp.full((nz, nz), -nz, jnp.int32)
    for k in range(levels):
        start_of = jnp.where(target == owner[k], k * zblock, start_of)
    gap = fine - 2 * (start_of + column % zblock)
    weight = jnp.where(
        gap == 0, 0.5, jnp.where((gap == 1) | (gap == -1), 0.25, 0.0)
    ).astype(jnp.bfloat16)
    rows_x[...] = jnp.zeros_like(rows_x)
    rows_b[...] = jnp.zeros_like(rows_b)
    beyond[...] = jnp.zeros_like(beyond)
    high_x, low_x = (in_halo[1, i, halo : halo + ny] for i in (0, 1))
    high_y, low_y = (in_halo[1, i, halo : halo + nx] for i in (2, 3))

    def restrict_x(target, f, cut):
        for k in range(-1, half_x + 1):
            value = 0.0
            for x, factor in ((2 * k - 1, 0.25), (2 * k, 0.5), (2 * k + 1, 0.25)):
                if x in cut:
                    value = value + factor * cut[x]
            if k >= 0 or -1 in cut:
                spot = (f * width + k + 1) * ny
                target[spot : spot + ny] = value

    for f in range(fields):
        res = jnp.where(keep, part[f * plane : (f + 1) * plane], 0.0)
        cut = {x: res[x * ny : (x + 1) * ny] for x in range(nx)}
        at = f * plane
        cut[-1] = low_x * cells[at : at + ny]
        cut[nx] = high_x * cells[at + plane - ny : at + plane]
        restrict_x(rows_x, f, cut)
        beyond[pl.ds(at, nx, stride=ny), :] = low_y * cells[pl.ds(at, nx, stride=ny), :]
        beyond[pl.ds(at + 1, nx, stride=ny), :] = (
            high_y * cells[pl.ds(at + ny - 1, nx, stride=ny), :]
        )
        restrict_x(
            rows_b, f, {x: beyond[at + x * ny : at + (x + 1) * ny] for x in range(nx)}
        )
    line = {y: rows_x[pl.ds(y, pad, stride=ny), :] for y in range(ny)}
    line[-1] = rows_b[pl.ds(0, pad, stride=ny), :]
    line[ny] = rows_b[pl.ds(1, pad, stride=ny), :]
    groups = []
    for k in [*range(half_y + 1), -1]:
        value = 0.0
        for y, factor in ((2 * k - 1, 0.25), (2 * k, 0.5), (2 * k + 1, 0.25)):
            if y in line:
                value = value + factor * line[y]
        groups.append(value)
    stacked = jnp.concatenate(groups, 0)
    high = stacked.astype(jnp.bfloat16)
    low = (stacked - high.astype(jnp.float32)).astype(jnp.bfloat16)
    product = jnp.dot(high, weight, preferred_element_type=jnp.float32) + jnp.dot(
        low, weight, preferred_element_type=jnp.float32
    )
    spot_of = lax.broadcasted_iota(jnp.int32, (pad, nz), 1) // zblock
    for d in range(levels):
        total = jnp.zeros((pad, nz), jnp.float32)
        for k in range(half_y):
            shift = ((k - d) * zblock) % nz
            moved = product[k * pad : (k + 1) * pad]
            if shift:
                moved = pltpu.roll(moved, shift, 1)
            total = jnp.where(spot_of == k, moved, total)
        packed[d] = total
        for side in range(2):
            total = jnp.zeros((8, nz), jnp.float32)
            for k in range(pad // 8):
                at = (half_y + side) * pad + k * 8
                moved = product[at : at + 8]
                shift = ((k - d) * zblock) % nz
                if shift:
                    moved = pltpu.roll(moved, shift, 1)
                total = jnp.where(spot_of[:8] == k, moved, total)
            packed_edge[side, d] = total

    def end_copy(k, edge):
        to = lax.rem(l + k, levels)
        return pltpu.make_async_remote_copy(
            src_ref=packed_edge.at[edge - 1, to] if edge else packed.at[to],
            dst_ref=(got, got_edge, got_low)[edge].at[l],
            send_sem=end_send.at[edge, k],
            recv_sem=end_recv.at[edge, k],
            device_id=(b + (0, 1, -1)[edge], to),
            device_id_type=MESH,
        )

    def end_arrival(k, edge):
        origin = lax.rem(l + levels - k, levels)
        return pltpu.make_async_remote_copy(
            src_ref=packed_edge.at[edge - 1, l] if edge else packed.at[l],
            dst_ref=(got, got_edge, got_low)[edge].at[origin],
            send_sem=end_send.at[edge, k],
            recv_sem=end_recv.at[edge, k],
            device_id=(b, origin),
            device_id_type=MESH,
        )

    @pl.when(has[2])
    def _():
        for k in range(levels):
            end_copy(k, 1).start()

    @pl.when(has[3])
    def _():
        for k in range(levels):
            end_copy(k, 2).start()

    for k in range(1, levels):
        end_copy(k, 0).start()
    got[l] = packed[l]
    store.wait()
    for e in range(SWEEPS):
        for i in range(4):

            @pl.when(can_send[i])
            def _():
                halo_copy(e, i).wait_send()

    for k in range(1, levels):
        end_arrival(k, 0).wait_recv()

    @pl.when(has[3])
    def _():
        for k in range(levels):
            end_arrival(k, 1).wait_recv()

    @pl.when(has[2])
    def _():
        for k in range(levels):
            end_arrival(k, 2).wait_recv()

    for s in range(levels):
        for k in range(pad // 8):
            first = pltpu.roll(got_edge[s], (-k * zblock) % nz, 1)
            last = pltpu.roll(got_low[s], ((half_y - 1 - k) * zblock) % nz, 1)
            mine = slice(k * 8, k * 8 + 8)
            merged[s, mine] = (
                got[s, mine]
                + jnp.where(spot_of[:8] == 0, first, 0.0)
                + jnp.where(spot_of[:8] == half_y - 1, last, 0.0)
            )
    for f in range(fields):
        at = f * width
        for s in range(levels):
            to = s * half_x
            coarse[f, to : to + half_x] = merged[s, at + 1 : at + 1 + half_x]
        for s in range(1, levels):
            to = s * half_x
            coarse[f, to : to + 1] += merged[s - 1, at + width - 1 : at + width]
            coarse[f, to - 1 : to] += merged[s, at : at + 1]

    for k in range(1, levels):
        end_copy(k, 0).wait_send()

    @pl.when(has[2])
    def _():
        for k in range(levels):
            end_copy(k, 1).wait_send()

    @pl.when(has[3])
    def _():
        for k in range(levels):
            end_copy(k, 2).wait_send()


def shards(bricks, levels, adjoint, source, block, precond, couple, solid, coarse_owner):
    fields, nx, ny, nz = adjoint.shape
    plane = nx * ny
    zblock = nz // (2 * levels)
    half_x, half_y = nx // 2, ny // 2
    pad = -(-fields * (half_x + 2) // 8) * 8
    flat = fields * plane
    halo = fields * max(nx, ny)
    f32, bf16 = jnp.float32, jnp.bfloat16
    vmem, dma = pltpu.VMEM, pltpu.SemaphoreType.DMA
    anywhere = pl.BlockSpec(memory_space=pltpu.HBM)
    cells, coarse = pl.pallas_call(
        functools.partial(kernel, bricks, levels, fields, nx, ny, zblock),
        out_shape=(
            jax.ShapeDtypeStruct((flat, nz), f32),
            vmem((fields, levels * half_x, nz), f32),
        ),
        in_specs=[anywhere] * 7,
        out_specs=(anywhere, pl.BlockSpec(memory_space=pltpu.VMEM)),
        scratch_shapes=[
            pltpu.SMEM((levels,), jnp.int32),
            vmem((flat, nz), f32),
            vmem((flat, nz), f32),
            vmem((fields * fields, plane, nz), bf16),
            vmem((fields * fields, plane, nz), bf16),
            vmem((fields * fields, plane, nz), f32),
            vmem((fields * fields, plane, nz), f32),
            vmem((3 * plane, nz), f32),
            vmem((plane, nz), jnp.int32),
            vmem((4, plane, nz), f32),
            vmem((flat, nz), f32),
            vmem((SWEEPS, 4, halo + max(nx, ny), nz), f32),
            vmem((SWEEPS, 4, halo + max(nx, ny), nz), f32),
            vmem((flat, nz), f32),
            vmem((pad * ny, nz), f32),
            vmem((pad * ny, nz), f32),
            vmem((levels, pad, nz), f32),
            vmem((2, levels, 8, nz), f32),
            vmem((2, fields * fields, nx, nz), f32),
            vmem((levels, pad, nz), f32),
            vmem((levels, 8, nz), f32),
            vmem((levels, 8, nz), f32),
            vmem((levels, pad, nz), f32),
            dma((7,)),
            dma,
            dma((SWEEPS, 4)),
            dma((SWEEPS, 4)),
            dma((3, levels)),
            dma((3, levels)),
        ],
        compiler_params=pltpu.CompilerParams(
            collective_id=0, has_side_effects=True, vmem_limit_bytes=60 * 1024 * 1024
        ),
    )(
        coarse_owner,
        adjoint.reshape(flat, nz),
        source.reshape(flat, nz),
        block.reshape(fields * fields, plane, nz),
        precond.reshape(fields * fields, plane, nz),
        couple.reshape(3 * plane, nz),
        solid.reshape(plane, nz),
    )
    rhs = coarse[:, :, : half_y * zblock].reshape(
        1, fields, levels * half_x, half_y, zblock
    )
    return cells.reshape(adjoint.shape), rhs


def solution(mesh):
    cells = P(None, "level", "brick", None)
    blocks = P(None, None, "level", "brick", None)
    return jax.shard_map(
        functools.partial(shards, mesh.shape["brick"], mesh.shape["level"]),
        mesh=mesh,
        in_specs=(cells, cells, blocks, blocks, cells, P("level", "brick", None), P()),
        out_specs=(cells, P("level", None, None, "brick", None)),
        check_vma=False,
    )
```
